128 devices in a mesh: expert: 8 (over y, x_lo), etp: 16 (over x_hi, z, core).
Axes of the slice: x: 4 (x_hi: 2, x_lo: 2; x = x_hi * 2 + x_lo), y: 4, z: 4, core: 2. Of those that a mesh axis runs over, the one named last changes fastest.
Arguments:
- tokens: bfloat16 [1024, 6144], P(('expert', 'etp')), may hold values from -6 to 6
- expert_ids: int32 [1024, 4], P('expert'), may hold values from 0 to 7, all different within a row; in each aligned block of 128 rows (0 to 127, 128 to 255, ...) at most 80 rows name the same one
- gate_values: float32 [1024, 4], P('expert'), may hold values from 0.1 to 1
- out_grad: bfloat16 [1024, 6144], P(('expert', 'etp')), may hold values from -1.1953125 to 1.1953125
- gate_weight: bfloat16 [8, 6144, 5376], P('expert', None, 'etp'), may hold values from -0.078125 to 0.078125
- up_weight: bfloat16 [8, 6144, 5376], P('expert', None, 'etp'), may hold values from -0.078125 to 0.078125
- down_weight: bfloat16 [8, 5376, 6144], P('expert', 'etp'), may hold values from -0.078125 to 0.078125
Outputs:
- grad_tokens: bfloat16 [1024, 6144], P('expert', 'etp')
- grad_gates: float32 [1024, 4], P('expert')
- grad_gate_weight: bfloat16 [8, 6144, 5376], P('expert', None, 'etp')
- grad_up_weight: bfloat16 [8, 6144, 5376], P('expert', None, 'etp')
- grad_down_weight: bfloat16 [8, 5376, 6144], P('expert', 'etp')
The draws below stay inside these ranges and needn't reach their ends.
Inputs may be any that keep to these rules, and one draw needn't show every extreme that they name: `expert_ids`: each row names 4 different experts. Among the 128 rows of one index of expert (aligned blocks), no expert is named by more than 80 rows, and in some block one expert is named by exactly 80 rows.
All inputs are finite; a program needn't handle non-finite values.
Results may differ from the reference program's by a relative error of at most 0.007.
Values may be sent and summed in bfloat16 or wider, within the bound.
No kernel may reach another device: no remote copies, remote signals or barrier semaphores. Data moves between devices by JAX's collectives and lax.ppermute only.
A program may use at most 192 MiB of HBM per device.

```python
import math
import jax
import jax.numpy as jnp
import numpy as np
from jax import lax

D = 6144
FF = 5376
TOP = 4
TOK_DEV = 128
EXPERTS = 8
TOKENS = 1024
MOST = 80
CAP = 640


def levels(key, extent, shards, smallest, largest):
    def one(position, parts):
        steps = jax.random.uniform(jax.random.fold_in(jax.random.fold_in(key, 6), position), (parts,), jnp.float32, smallest / len(shards), largest / len(shards))
        return jnp.repeat(jnp.exp(steps), extent[position] // parts).reshape((-1,) + (1,) * (len(extent) - position - 1))

    gain = one(*shards[0])
    for cut in shards[1:]:
        gain = gain * one(*cut)
    return gain


def routed_block(own_key, own, number, rows, amount, top, reach, lean):
    ranking = jax.random.permutation(own_key, amount)
    packed, usual = load_shares(amount, rows * top, reach, lean, True), load_shares(amount, rows * top, reach, lean, False)
    places = jnp.arange(amount)

    def named(tallies, offset_by):
        used = int((tallies > 0).sum())
        fixed = max(1, used // 4)
        moved = fixed + (places - fixed + offset_by * (used - fixed)) % max(1, amount - fixed)
        return jnp.zeros((amount,), jnp.int32).at[ranking[jnp.where(places < fixed, places, moved)]].set(jnp.asarray(tallies, jnp.int32))

    tallies = jnp.where(number % 4 == 0, named(packed, number // 4), named(usual, number - number // 4 - 1))
    mixed = jax.random.permutation(jax.random.fold_in(own, 3), amount)
    giver, receiver = mixed[0:amount // 2 * 2:2], mixed[1:amount // 2 * 2:2]
    margin = jnp.minimum(tallies[giver] - 1, reach - tallies[receiver]) // 2
    margin = jnp.where((giver == ranking[0]) | (receiver == ranking[0]) | (tallies[receiver] == 0), 0, jnp.maximum(margin, 0))
    moved = jax.random.randint(jax.random.fold_in(own, 4), (amount // 2,), 0, 1 << 20) % (margin + 1)
    tallies = tallies.at[giver].add(-moved).at[receiver].add(moved)
    items = jnp.searchsorted(jnp.cumsum(tallies), jnp.arange(rows * top), side="right").astype(jnp.int32)
    grid = items.reshape(top, rows).T
    grid = grid[jax.random.permutation(jax.random.fold_in(own, 1), rows)]
    offset_by = jax.random.randint(jax.random.fold_in(own, 2), (rows, 1), 0, top)
    return jnp.take_along_axis(grid, (jnp.arange(top)[None, :] + offset_by) % top, axis=1)


def load_shares(count, total, most, skew, full):
    weights = [(1 << 20) // math.isqrt(standing ** skew) + 1 for standing in range(1, count + 1)]
    largest = most if full else min(most, max(-(-total // count), total * weights[0] // sum(weights)))
    least = 1 if total - largest >= count - 1 else 0
    holding, spare = [largest] + [least] * (count - 1), total - largest - least * (count - 1)
    while spare > 0:
        candidates = [i for i in range(1, count) if holding[i] < largest] or [i for i in range(1, count) if holding[i] < most]
        mass, left = sum([weights[i] for i in candidates]), spare
        for i in candidates:
            more = min(most - holding[i], max(1, left * weights[i] // mass), spare)
            holding[i] = holding[i] + more
            spare = spare - more
    return np.array(holding)


def gaussian(stream_key, dims, spread, most, split=(), kind=jnp.bfloat16):
    level = levels(stream_key, dims, split, -0.22, 0.18) if split else 1.0
    result = jax.random.normal(stream_key, dims, jnp.float32) * spread * level
    return jnp.minimum(jnp.maximum(result, -most), most).astype(kind)


def setup_inputs(seed: int = 0) -> dict:
    key_list = jax.random.split(jax.random.key(seed), 8)
    tokens = gaussian(key_list[0], (TOKENS, D), 1.0, 6.0, ((0, 128),))
    expert_ids_keys = jax.random.split(jax.random.fold_in(key_list[1], 1), TOKENS // TOK_DEV)
    expert_ids_turns = jax.random.permutation(jax.random.fold_in(key_list[1], 3), TOKENS // TOK_DEV)
    expert_ids = jax.vmap(lambda own, number: routed_block(jax.random.fold_in(key_list[1], 2), own, number, TOK_DEV, EXPERTS, TOP, MOST, 2))(expert_ids_keys, expert_ids_turns).reshape((TOKENS, TOP))
    gate_values = jnp.clip(0.1 + 0.9 * jax.random.uniform(key_list[2], (TOKENS, TOP), jnp.float32) ** levels(key_list[2], (TOKENS, TOP), ((0, 8),), -0.2, 0.2), 0.1, 1.0)
    out_grad = gaussian(key_list[3], (TOKENS, D), 0.2, 1.1953125, ((0, 128),))
    gate_weight = gaussian(key_list[4], (EXPERTS, D, FF), D ** -0.5, 0.078125, ((0, 8), (2, 16)))
    up_weight = gaussian(key_list[5], (EXPERTS, D, FF), D ** -0.5, 0.078125, ((0, 8), (2, 16)))
    down_weight = gaussian(key_list[6], (EXPERTS, FF, D), FF ** -0.5, 0.078125, ((0, 8), (1, 16)))
    return {"tokens": tokens, "expert_ids": expert_ids, "gate_values": gate_values, "out_grad": out_grad, "gate_weight": gate_weight, "up_weight": up_weight, "down_weight": down_weight}


def expert_grads(rows_in, rows_grad, weights, gate_weight, up_weight, down_weight):
    gate_pre = jnp.dot(rows_in, gate_weight, preferred_element_type=jnp.float32)
    up_pre = jnp.dot(rows_in, up_weight, preferred_element_type=jnp.float32)
    sigmoid_gate = jax.nn.sigmoid(gate_pre)
    active = gate_pre * sigmoid_gate
    hidden = (active * up_pre).astype(jnp.bfloat16)
    scaled = (weights[:, None] * rows_grad.astype(jnp.float32)).astype(jnp.bfloat16)
    raw_grad = lax.dot_general(rows_grad, down_weight, (((1,), (1,)), ((), ())), preferred_element_type=jnp.float32)
    gate_terms = jnp.sum(hidden.astype(jnp.float32) * raw_grad, axis=1)
    hidden_grad = weights[:, None] * raw_grad
    grad_gate_pre = (hidden_grad * up_pre * sigmoid_gate * (1.0 + gate_pre * (1.0 - sigmoid_gate))).astype(jnp.bfloat16)
    grad_up_pre = (hidden_grad * active).astype(jnp.bfloat16)
    down_grad = lax.dot_general(hidden, scaled, (((0,), (0,)), ((), ())), preferred_element_type=jnp.float32).astype(jnp.bfloat16)
    gate_grad = lax.dot_general(rows_in, grad_gate_pre, (((0,), (0,)), ((), ())), preferred_element_type=jnp.float32).astype(jnp.bfloat16)
    up_grad = lax.dot_general(rows_in, grad_up_pre, (((0,), (0,)), ((), ())), preferred_element_type=jnp.float32).astype(jnp.bfloat16)
    input_grad = lax.dot_general(grad_gate_pre, gate_weight, (((1,), (1,)), ((), ())), preferred_element_type=jnp.float32)
    input_grad = input_grad + lax.dot_general(grad_up_pre, up_weight, (((1,), (1,)), ((), ())), preferred_element_type=jnp.float32)
    return input_grad, gate_terms, gate_grad, up_grad, down_grad


def reference(tokens, expert_ids, gate_values, out_grad, gate_weight, up_weight, down_weight):
    def expert_step(totals, inputs):
        input_total, gate_total = totals
        target, weight_gate, weight_up, weight_down = inputs
        chosen = expert_ids == target
        routed = jnp.any(chosen, axis=1).astype(jnp.int32)
        slot_order = jnp.argsort(1 - routed, stable=True)[:CAP].astype(jnp.int32)
        picked = chosen[slot_order].astype(jnp.float32)
        weights = jnp.sum(gate_values[slot_order] * picked, axis=1)
        results = expert_grads(tokens[slot_order], out_grad[slot_order], weights, weight_gate, weight_up, weight_down)
        input_total = input_total.at[slot_order].add(results[0])
        gate_total = gate_total.at[slot_order].add(results[1][:, None] * picked)
        return (input_total, gate_total), (results[2], results[3], results[4])

    start = (jnp.zeros((TOKENS, D), jnp.float32), jnp.zeros((TOKENS, TOP), jnp.float32))
    targets = jnp.arange(EXPERTS, dtype=jnp.int32)
    (input_total, gate_total), grads = lax.scan(expert_step, start, (targets, gate_weight, up_weight, down_weight))
    return input_total.astype(jnp.bfloat16), gate_total, grads[0], grads[1], grads[2]
```

```python
import jax
import jax.numpy as jnp
from jax import lax
from jax.experimental import pallas as pl
from jax.experimental.pallas import tpu as pltpu
from jax.sharding import PartitionSpec as P

BF16 = jnp.bfloat16
F32 = jnp.float32
VMEM_LIMIT = 56 * 1024 * 1024
GAP = 384
SPARE = 16
BRIEF = pl.CostEstimate(flops=1, bytes_accessed=1, transcendentals=0)
PLACES = ((0, 0), (0, 1), (0, -1), (1, 0), (0, 2), (1, 1), (1, -1), (1, 2))


def etp_index(x, z, core):
    return x * 8 + (z % 4) * 2 + core


def etp_moves(flip_x, step_z, flip_core):
    return [
        (etp_index(x, z, c), etp_index(x ^ flip_x, z + step_z, c ^ flip_core))
        for x in range(2)
        for z in range(4)
        for c in range(2)
    ]


CORE = etp_moves(0, 0, 1)
UP = etp_moves(0, 1, 0)
DOWN = etp_moves(0, -1, 0)
ACROSS = etp_moves(1, 0, 0)


def move(value, moves):
    return lax.ppermute(value, "etp", moves)


def tie(first, *others):
    return lax.optimization_barrier((first, *others))


def add(*terms):
    total = terms[0].astype(F32)
    for term in terms[1:]:
        total = total + term.astype(F32)
    return total


def parts_of(value):
    high = lax.reduce_precision(value, 8, 7)
    rest = value - high
    middle = lax.reduce_precision(rest, 8, 7)
    return [part.astype(BF16) for part in (high, middle, rest - middle)]


def gather_near(chunk, local):
    half = chunk.shape[0] // 2
    from_below, from_above, across = move(chunk, UP), move(chunk, DOWN), move(chunk, ACROSS)
    beside = move(chunk, CORE)
    from_below, from_above, across, beside, local = tie(from_below, from_above, across, beside, local(chunk))
    onward = (
        move(from_below[:half], UP),
        move(from_above[half:], DOWN),
        move(across, DOWN),
        move(across, UP),
    )
    mine = [chunk, from_above, from_below, across]
    return mine, [beside] + [move(part, CORE) for part in mine[1:]], onward, local


def begin(groups, now):
    for group in groups[:2] if now < 0 else groups[now + 2 : now + 3]:
        for copy in group:
            copy.start()


def finish(group):
    for copy in group:
        copy.wait()


def column_blocks(place_ref, at, width):
    core = place_ref[8]
    first = place_ref[at] * 2
    return [pl.ds(pl.multiple_of((first + side) * width, 128), width) for side in (core, 1 - core)]


def dense_kernel(first, count, last, place_ref, *refs):
    chunks, refs = (refs[:count], refs[count : 2 * count]), refs[2 * count :]
    weights, refs = refs[:3], refs[3:]
    if first:
        both_before_ref, raw_before_ref, refs = refs[0], refs[1], refs[2:]
    if last:
        weight_ref, grads_ref, hidden_ref, mine_ref, other_ref = refs[:5]
        both_ref, raw_ref, sums_ref, terms_buf, terms_sem, near_sem = refs[5:11]
        refs = refs[11:]
    else:
        both_ref, raw_ref = refs[:2]
        refs = refs[2:]
    rows_buf, out_buf, both_buf, down_buf, sem = refs
    width = chunks[0][0].shape[1] // 2
    units = weights[0].shape[0]
    loads = []
    for j in range(count):
        pairs = []
        for side, block in enumerate(column_blocks(place_ref, first + j, width)):
            to = pl.ds(side * width, width)
            pairs.append((weights[0].at[:, block], both_buf.at[j, pl.ds(0, units), to]))
            pairs.append((weights[1].at[:, block], both_buf.at[j, pl.ds(GAP, units), to]))
            pairs.append((weights[2].at[:, block], down_buf.at[j, :, to]))
            pairs.append((chunks[side][j].at[:, pl.ds(0, width)], rows_buf.at[j, :, to]))
            pairs.append((chunks[side][j].at[:, pl.ds(width, width)], out_buf.at[j, :, to]))
        loads.append([pltpu.make_async_copy(s, d, sem.at[j, k]) for k, (s, d) in enumerate(pairs)])
    begin(loads, -1)
    nears = []
    if last:
        for j in range(first):
            pairs = []
            for side, block in enumerate(column_blocks(place_ref, j, width)):
                to = pl.ds(side * width, width)
                pairs.append((weights[0].at[:, block], both_buf.at[count + j, pl.ds(0, units), to]))
                pairs.append((weights[1].at[:, block], both_buf.at[count + j, pl.ds(GAP, units), to]))
            nears.append([pltpu.make_async_copy(s, d, near_sem.at[j, k]) for k, (s, d) in enumerate(pairs)])
    blank = jnp.zeros((both_buf.shape[0], GAP - units, 2 * width), BF16)
    both_buf[:, units:GAP, :] = blank
    both_buf[:, GAP + units :, :] = blank
    across = (((1,), (1,)), ((), ()))
    for j in range(count):
        finish(loads[j])
        begin(loads, j)
        both_part = lax.dot_general(rows_buf[j], both_buf[j], across, preferred_element_type=F32)
        raw_part = lax.dot_general(out_buf[j], down_buf[j], across, preferred_element_type=F32)
        if j:
            both_ref[...] += both_part
            raw_ref[...] += raw_part
        elif first:
            both_ref[...] = both_before_ref[...] + both_part
            raw_ref[...] = raw_before_ref[...] + raw_part
        else:
            both_ref[...] = both_part
            raw_ref[...] = raw_part

    if last:
        for group in nears:
            for copy in group:
                copy.start()
        step = 80

        @pl.loop(0, raw_ref.shape[0] // step)
        def _(i):
            rows = pl.ds(pl.multiple_of(i * step, step), step)
            gate, up, raw = both_ref[rows, :units], both_ref[rows, GAP : GAP + units], raw_ref[rows, :]
            weight = weight_ref[rows, :]
            sigmoid = jax.nn.sigmoid(gate)
            active = gate * sigmoid
            hidden = (active * up).astype(BF16)
            hidden_ref[rows, :] = hidden
            sums_ref[rows, :] = jnp.sum(hidden.astype(F32) * raw, axis=1, keepdims=True)
            hidden_grad = weight * raw
            grad_gate = hidden_grad * up * sigmoid * (1.0 + gate * (1.0 - sigmoid))
            nothing = jnp.zeros((step, GAP - units), BF16)
            grads_ref[rows, units:GAP] = nothing
            grads_ref[rows, GAP + units :] = nothing
            grads_ref[rows, :units] = grad_gate.astype(BF16)
            grads_ref[rows, GAP : GAP + units] = (hidden_grad * active).astype(BF16)

        stores = []
        for j in range(count + first):
            if j >= count:
                finish(nears[j - count])
            for i in range(terms_buf.shape[1] // 2):
                rows = pl.ds(2 * i * step, 2 * step)
                total = jnp.dot(grads_ref[rows, :], both_buf[j], preferred_element_type=F32).astype(BF16)
                terms_buf[j, 2 * i, :step, :] = total[:step]
                terms_buf[j, 2 * i + 1, :step, :] = total[step:]
            for i in range(terms_buf.shape[1]):
                if j == 0:
                    spare_rows(sums_ref, i * step, step, terms_buf.at[j, i], width)
                else:
                    terms_buf[j, i, step:, :] = terms_buf[0, i, step:, :]
            to = place_ref[(first + j) % 8]
            group = [
                pltpu.make_async_copy(
                    terms_buf.at[j, :, :, pl.ds(side * width, width)], out.at[:, to], terms_sem.at[j, side]
                )
                for side, out in enumerate((mine_ref, other_ref))
            ]
            for copy in group:
                copy.start()
            stores.append(group)
        for group in stores:
            finish(group)


def spare_rows(sums_ref, start, count, out_ref, width):
    lane = lax.broadcasted_iota(jnp.int32, (SPARE, 128), 1)
    tile = jnp.zeros((SPARE, 128), F32)
    for g in range(count // SPARE):
        rest = sums_ref[pl.ds(start + g * SPARE, SPARE), :]
        for part in range(3):
            piece = rest.astype(BF16).astype(F32)
            tile = jnp.where(lane == part * 8 + g, piece, tile)
            rest = rest - piece
    out_ref[pl.ds(count, SPARE), :] = jnp.zeros((SPARE, 2 * width), BF16)
    out_ref[pl.ds(count, SPARE), pl.ds(0, 128)] = tile.astype(BF16)
    out_ref[pl.ds(count, SPARE), pl.ds(width + 128, 128)] = tile.astype(BF16)


IN_HBM = pl.BlockSpec(memory_space=pl.ANY)
IN_VMEM = pl.BlockSpec(memory_space=pltpu.VMEM)
IN_SMEM = pl.BlockSpec(memory_space=pltpu.SMEM)


def dense(place, first, mine, other, weights, before, scale=None, groups=None):
    last = scale is not None
    rows, both = mine[0].shape
    units, depth = weights[0].shape
    count = len(mine)
    totals = [(rows, 2 * GAP), (rows, units)]
    shapes = [jax.ShapeDtypeStruct(s, F32) for s in totals]
    kept, carried, held = [], before, count
    if last:
        held, span = count + first, rows // groups + SPARE
        terms = jax.ShapeDtypeStruct((groups, held, span, both // 2), BF16)
        shapes = [
            jax.ShapeDtypeStruct((rows, 2 * GAP), BF16),
            jax.ShapeDtypeStruct((rows, units), BF16),
            terms,
            terms,
        ]
        kept = [pltpu.VMEM(s, F32) for s in totals] + [
            pltpu.VMEM((rows, 1), F32),
            pltpu.VMEM((held, groups, span, both), BF16),
            pltpu.SemaphoreType.DMA((held, 2)),
            pltpu.SemaphoreType.DMA((first, 4)),
        ]
        carried = (*before, scale)
    return pl.pallas_call(
        lambda *refs: dense_kernel(first, count, last, *refs),
        out_shape=tuple(shapes),
        in_specs=[IN_SMEM] + [IN_HBM] * (2 * count + 3) + [IN_VMEM] * len(carried),
        out_specs=[IN_VMEM] * 2 + [IN_HBM] * (2 if last else 0),
        scratch_shapes=kept
        + [
            pltpu.VMEM((count, rows, both), BF16),
            pltpu.VMEM((count, rows, both), BF16),
            pltpu.VMEM((held, 2 * GAP, both), BF16),
            pltpu.VMEM((count, units, both), BF16),
            pltpu.SemaphoreType.DMA((count, 10)),
        ],
        compiler_params=pltpu.CompilerParams(vmem_limit_bytes=VMEM_LIMIT),
        cost_estimate=BRIEF,
        name="dense",
    )(place, *mine, *other, *weights, *carried)


def weight_kernel(place_ref, *refs):
    chunks, refs = (refs[:8], refs[8:16]), refs[16:]
    lefts, scale_ref, outs = refs[:2], refs[2], (refs[3:5], refs[5:6])
    rows_buf, both_buf, down_buf, sem, out_sem = refs[6:]
    width = chunks[0][0].shape[1] // 2
    units = outs[0][0].shape[0]
    loads, stores = [], []
    for part, out_buf in enumerate((both_buf, down_buf)):
        for j in range(8):
            load, store = [], []
            for side, block in enumerate(column_blocks(place_ref, j, width)):
                to = pl.ds(side * width, width)
                source = chunks[side][j].at[:, pl.ds(part * width, width)]
                load.append(pltpu.make_async_copy(source, rows_buf.at[part, j, :, to], sem.at[part, j, side]))
                for k, out in enumerate(outs[part]):
                    result = out_buf.at[j, pl.ds(k * GAP, units), to]
                    store.append(
                        pltpu.make_async_copy(result, out.at[:, block], out_sem.at[part, j, 2 * side + k])
                    )
            loads.append(load)
            stores.append(store)
    begin(loads, -1)
    for part, out_buf in enumerate((both_buf, down_buf)):
        step = out_buf.shape[1] // 3
        for j in range(8):
            finish(loads[8 * part + j])
            begin(loads, 8 * part + j)
            if part:
                rows_buf[1, j] = (scale_ref[...] * rows_buf[1, j].astype(F32)).astype(BF16)
            for i in range(3):
                at = pl.ds(i * step, step)
                total = jnp.dot(lefts[part][at, :], rows_buf[part, j], preferred_element_type=F32)
                out_buf[j, at, :] = total.astype(BF16)
            for copy in stores[8 * part + j]:
                copy.start()
    for group in stores:
        finish(group)


def weight_grads(place, mine, other, grads, hidden, scale):
    rows, both = mine[0].shape
    units = hidden.shape[0]
    shape = jax.ShapeDtypeStruct((units, 8 * both), BF16)
    return pl.pallas_call(
        weight_kernel,
        out_shape=(shape,) * 3,
        in_specs=[IN_SMEM] + [IN_HBM] * 16 + [IN_VMEM] * 3,
        out_specs=[IN_HBM] * 3,
        scratch_shapes=[
            pltpu.VMEM((2, 8, rows, both), BF16),
            pltpu.VMEM((8, GAP + units, both), BF16),
            pltpu.VMEM((8, units, both), BF16),
            pltpu.SemaphoreType.DMA((2, 8, 2)),
            pltpu.SemaphoreType.DMA((2, 8, 4)),
        ],
        compiler_params=pltpu.CompilerParams(vmem_limit_bytes=VMEM_LIMIT),
        cost_estimate=BRIEF,
        name="weight_grads",
    )(place, *mine, *other, grads, hidden, scale)


def shards(tokens, expert_ids, gate_values, out_grad, gate_weight, up_weight, down_weight):
    groups, lanes = lax.axis_size("expert"), lax.axis_size("etp")
    block_rows, top_count = expert_ids.shape
    own_rows, depth = tokens.shape
    width = depth // lanes
    most_rows = min(block_rows, 5 * block_rows * top_count // (4 * groups))
    capacity = groups * most_rows
    gate_weight, up_weight, down_weight = gate_weight[0], up_weight[0], down_weight[0]

    me = lax.axis_index("etp")
    x, z, core = me // 8, (me // 2) % 4, me % 2
    place = jnp.stack([(x ^ fx) * 4 + (z + sz) % 4 for fx, sz in PLACES]).astype(jnp.int32)

    chosen = expert_ids[:, :, None] == jnp.arange(groups, dtype=jnp.int32)
    routed = jnp.any(chosen, axis=1)
    share = jnp.sum(jnp.where(chosen, gate_values[:, :, None], 0.0), axis=1)
    earlier = jnp.tril(jnp.ones((block_rows, block_rows), BF16), -1)
    slot = jnp.dot(earlier, routed.astype(BF16), preferred_element_type=F32).astype(jnp.int32)
    slot = jnp.where(routed, slot, -1)
    fills = slot.T[:, None, :] == jnp.arange(most_rows, dtype=jnp.int32)[None, :, None]
    slot_weights = jnp.sum(jnp.where(fills, share.T[:, None, :], 0.0), axis=2)
    pick = fills.astype(BF16).reshape(capacity, block_rows)

    both = jnp.concatenate(
        [tokens.reshape(own_rows, lanes, width), out_grad.reshape(own_rows, lanes, width)], axis=2
    )
    columns = lax.all_to_all(both.transpose(1, 0, 2), "etp", 0, 0)
    columns = columns.reshape(block_rows, 2 * width)
    packed = jnp.dot(pick, columns, preferred_element_type=F32).astype(BF16)
    received = lax.all_to_all(packed.reshape(groups, most_rows, 2 * width), "expert", 0, 0)
    received = received.reshape(capacity, 2 * width)

    def weights_of(chunk):
        parts = jnp.pad(jnp.stack(parts_of(slot_weights), axis=1), ((0, 0), (0, 13), (0, 128 - most_rows)))
        parts, _ = tie(parts, chunk)
        parts = lax.all_to_all(parts, "expert", 0, 0)[:, :3, :most_rows].astype(F32)
        return jnp.sum(parts, axis=1).reshape(capacity, 1)

    place = jnp.concatenate([place, core[None].astype(jnp.int32)])
    gate_weight, up_weight = gate_weight.T, up_weight.T
    every_weight = (gate_weight, up_weight, down_weight)
    near, near_other, onward, weights = gather_near(received, weights_of)
    sums = dense(place, 0, near, near_other, every_weight, ())
    far_low, far_high, across_above, across_below = onward
    far_low, far_high, *sums = tie(far_low, far_high, *sums)
    far = jnp.concatenate([far_low, far_high], axis=0)
    across_far, far_other = move(far, ACROSS), move(far, CORE)
    across_above, across_below, far_other = tie(across_above, across_below, far_other)
    distant = [far, across_above, across_below, across_far]
    distant_other = [far_other] + [move(part, CORE) for part in distant[1:]]
    grads, hidden, own_terms, other_terms = dense(
        place, 4, distant, distant_other, every_weight, sums, weights, groups
    )
    gate_grad, up_grad, down_grad = weight_grads(
        place, near + distant, near_other + distant_other, grads.T, hidden.T, weights
    )

    terms = add(own_terms, move(other_terms, CORE)).astype(BF16)
    terms = terms.reshape(groups * 8, most_rows + SPARE, width)
    peers = [[e * lanes + 2 * p + c for e in range(groups) for p in range(8)] for c in range(2)]
    back = lax.all_to_all(terms, ("expert", "etp"), 0, 0, axis_index_groups=peers)
    back = jnp.sum(back.reshape(groups, 8, most_rows + SPARE, width).astype(F32), axis=1)
    own_input = lax.dot_general(
        pick,
        back[:, :most_rows].astype(BF16).reshape(capacity, width),
        (((0,), (0,)), ((), ())),
        preferred_element_type=F32,
    ).astype(BF16)
    slot_sums = back[:, most_rows:, :256].reshape(groups, SPARE, 2, 16, 8)
    slot_sums = jnp.sum(slot_sums, axis=(2, 3))[:, :, : most_rows // SPARE]
    slot_sums = slot_sums.transpose(0, 2, 1).reshape(groups, most_rows, 1)
    token_sums = jnp.sum(jnp.where(fills, slot_sums, 0.0), axis=1)
    own_gates = jnp.sum(jnp.where(chosen, token_sums.T[:, None, :], 0.0), axis=2)
    return own_input, own_gates, gate_grad.T[None], up_grad.T[None], down_grad[None]


def solution(mesh):
    placed = (
        P(("expert", "etp"), None),
        P("expert", None),
        P("expert", None),
        P(("expert", "etp"), None),
        P("expert", None, "etp"),
        P("expert", None, "etp"),
        P("expert", "etp", None),
    )
    return jax.shard_map(
        shards,
        mesh=mesh,
        in_specs=placed,
        out_specs=(
            P("expert", "etp"),
            P("expert", None),
            P("expert", None, "etp"),
            P("expert", None, "etp"),
            P("expert", "etp", None),
        ),
        check_vma=False,
    )
```

```python
import jax
import jax.numpy as jnp
from jax import lax
from jax.experimental import pallas as pl
from jax.experimental.pallas import tpu as pltpu
from jax.sharding import PartitionSpec as P

BF16 = jnp.bfloat16
F32 = jnp.float32
VMEM_LIMIT = 56 * 1024 * 1024
GAP = 384
SPARE = 16
SUMS_AT = 80
BRIEF = pl.CostEstimate(flops=1, bytes_accessed=1, transcendentals=0)
PLACES = ((0, 0), (0, 1), (0, -1), (1, 0), (0, 2), (1, 1), (1, -1), (1, 2))


def etp_index(x, z, core):
    return x * 8 + (z % 4) * 2 + core


def etp_moves(flip_x, step_z, flip_core):
    return [
        (etp_index(x, z, c), etp_index(x ^ flip_x, z + step_z, c ^ flip_core))
        for x in range(2)
        for z in range(4)
        for c in range(2)
    ]


CORE = etp_moves(0, 0, 1)
UP = etp_moves(0, 1, 0)
DOWN = etp_moves(0, -1, 0)
ACROSS = etp_moves(1, 0, 0)


def move(value, moves):
    return lax.ppermute(value, "etp", moves)


def tie(first, *others):
    return lax.optimization_barrier((first, *others))


def parts_of(value):
    high = lax.reduce_precision(value, 8, 7)
    rest = value - high
    middle = lax.reduce_precision(rest, 8, 7)
    return [part.astype(BF16) for part in (high, middle, rest - middle)]


def gather_near(chunk, local):
    half = chunk.shape[0] // 2
    from_below, from_above, across = move(chunk, UP), move(chunk, DOWN), move(chunk, ACROSS)
    beside = move(chunk, CORE)
    from_below, from_above, across, beside, *local = tie(from_below, from_above, across, beside, *local(chunk))
    onward = (
        move(from_below[:half], UP),
        move(from_above[half:], DOWN),
        move(across, DOWN),
        move(across, UP),
    )
    mine = [chunk, from_above, from_below, across]
    return mine, [beside] + [move(part, CORE) for part in mine[1:]], onward, local


def begin(groups, now):
    for group in groups[:2] if now < 0 else groups[now + 2 : now + 3]:
        for copy in group:
            copy.start()


def finish(group):
    for copy in group:
        copy.wait()


def column_blocks(place_ref, at, width):
    core = place_ref[8]
    first = place_ref[at] * 2
    return [pl.ds(pl.multiple_of((first + side) * width, 128), width) for side in (core, 1 - core)]


def dense_kernel(first, count, last, place_ref, *refs):
    chunks, refs = (refs[:count], refs[count : 2 * count]), refs[2 * count :]
    weights, refs = refs[:3], refs[3:]
    if last:
        before, weight_ref, grads_ref, hidden_ref = refs[:2], refs[2], refs[3], refs[4]
        both_ref, raw_ref, before_sem = refs[5:8]
        refs = refs[8:]
    else:
        both_ref, raw_ref = refs[:2]
        refs = refs[2:]
    rows_buf, out_buf, both_buf, down_buf, sem = refs
    width = chunks[0][0].shape[1] // 2
    units = weights[0].shape[0]
    loads = []
    for j in range(count):
        pairs = []
        for side, block in enumerate(column_blocks(place_ref, first + j, width)):
            to = pl.ds(side * width, width)
            pairs.append((weights[0].at[:, block], both_buf.at[j, pl.ds(0, units), to]))
            pairs.append((weights[1].at[:, block], both_buf.at[j, pl.ds(GAP, units), to]))
            pairs.append((weights[2].at[:, block], down_buf.at[j, :, to]))
            pairs.append((chunks[side][j].at[:, pl.ds(0, width)], rows_buf.at[j, :, to]))
            pairs.append((chunks[side][j].at[:, pl.ds(width, width)], out_buf.at[j, :, to]))
        loads.append([pltpu.make_async_copy(s, d, sem.at[j, k]) for k, (s, d) in enumerate(pairs)])
    begin(loads, -1)
    if last:
        carried = [
            pltpu.make_async_copy(source, to, before_sem.at[k])
            for k, (source, to) in enumerate(zip(before, (both_ref, raw_ref)))
        ]
        for copy in carried:
            copy.start()
    blank = jnp.zeros((both_buf.shape[0], GAP - units, 2 * width), BF16)
    both_buf[:, units:GAP, :] = blank
    both_buf[:, GAP + units :, :] = blank
    across = (((1,), (1,)), ((), ()))
    for j in range(count):
        finish(loads[j])
        begin(loads, j)
        both_part = lax.dot_general(rows_buf[j], both_buf[j], across, preferred_element_type=F32)
        raw_part = lax.dot_general(out_buf[j], down_buf[j], across, preferred_element_type=F32)
        if last and j == 0:
            finish(carried)
        if last or j:
            both_ref[...] += both_part
            raw_ref[...] += raw_part
        else:
            both_ref[...] = both_part
            raw_ref[...] = raw_part

    if last:
        step = 80

        @pl.loop(0, raw_ref.shape[0] // step)
        def _(i):
            rows = pl.ds(pl.multiple_of(i * step, step), step)
            gate, up, raw = both_ref[rows, :units], both_ref[rows, GAP : GAP + units], raw_ref[rows, :]
            weight = weight_ref[rows, :]
            sigmoid = jax.nn.sigmoid(gate)
            active = gate * sigmoid
            hidden = (active * up).astype(BF16)
            hidden_ref[rows, :] = hidden
            rest = jnp.sum(hidden.astype(F32) * raw, axis=1, keepdims=True)
            lane = lax.broadcasted_iota(jnp.int32, (step, GAP - units), 1)
            sums = jnp.zeros((step, GAP - units), F32)
            for part in range(3):
                piece = rest.astype(BF16).astype(F32)
                sums = jnp.where(lane == part, piece, sums)
                rest = rest - piece
            hidden_grad = weight * raw
            grad_gate = hidden_grad * up * sigmoid * (1.0 + gate * (1.0 - sigmoid))
            grads_ref[rows, units:GAP] = jnp.zeros((step, GAP - units), BF16)
            grads_ref[rows, GAP + units :] = sums.astype(BF16)
            grads_ref[rows, :units] = grad_gate.astype(BF16)
            grads_ref[rows, GAP : GAP + units] = (hidden_grad * active).astype(BF16)


def terms_kernel(place_ref, grads_ref, other_grads_ref, gate_ref, up_ref, other_ref, out_ref, *scratch):
    grads_buf, weight_buf, terms_buf, grads_sem, sem, terms_sem = scratch
    width = out_ref.shape[3]
    units = gate_ref.shape[0]
    span = 2 * GAP
    core = place_ref[8]
    step = out_ref.shape[2] - SPARE
    both = [
        pltpu.make_async_copy(source, grads_buf.at[:, pl.ds(k * span, span)], grads_sem.at[k])
        for k, source in enumerate((grads_ref, other_grads_ref))
    ]
    for copy in both:
        copy.start()
    loads = []
    for j in range(4):
        pairs = []
        for side in range(2):
            block = pl.ds(pl.multiple_of((2 * (2 * j + side) + core) * width, 128), width)
            to = pl.ds(side * width, width)
            pairs.append((gate_ref.at[:, block], weight_buf.at[j, pl.ds(0, units), to]))
            pairs.append((up_ref.at[:, block], weight_buf.at[j, pl.ds(GAP, units), to]))
        block = pl.ds(2 * j * width, 2 * width)
        for k in range(2):
            rows = pl.ds(span + k * GAP, units)
            pairs.append((other_ref.at[pl.ds(k * units, units), block], weight_buf.at[j, rows, :]))
        loads.append([pltpu.make_async_copy(s, d, sem.at[j, k]) for k, (s, d) in enumerate(pairs)])
    begin(loads, -1)
    for k in range(4):
        weight_buf[:, k * GAP + units : (k + 1) * GAP, :] = jnp.zeros((4, GAP - units, 2 * width), BF16)
    finish(both)
    stores = []
    for j in range(4):
        finish(loads[j])
        begin(loads, j)
        for i in range(terms_buf.shape[1] // 2):
            rows = pl.ds(2 * i * step, 2 * step)
            total = jnp.dot(grads_buf[rows, :], weight_buf[j], preferred_element_type=F32).astype(BF16)
            terms_buf[j, 2 * i, :step, :] = total[:step]
            terms_buf[j, 2 * i + 1, :step, :] = total[step:]
        for i in range(terms_buf.shape[1]):
            terms_buf[j, i, step:, :] = jnp.zeros((SPARE, 2 * width), BF16)
            tile = spare_rows(grads_buf, i * step, step) if j == 0 else terms_buf[0, i, step:, :128]
            terms_buf[j, i, step:, :128] = tile
            terms_buf[j, i, step:, width : width + 128] = tile
        group = [
            pltpu.make_async_copy(
                terms_buf.at[j, :, :, pl.ds(side * width, width)], out_ref.at[:, 2 * j + side], terms_sem.at[j, side]
            )
            for side in range(2)
        ]
        for copy in group:
            copy.start()
        stores.append(group)
    for group in stores:
        finish(group)


def spare_rows(grads_buf, start, count):
    lane = lax.broadcasted_iota(jnp.int32, (SPARE, 128), 1)
    tile = jnp.zeros((SPARE, 128), F32)
    for k in range(2):
        end = 2 * GAP * (k + 1)
        for g in range(count // SPARE):
            parts = grads_buf[pl.ds(start + g * SPARE, SPARE), end - 128 : end].astype(F32)
            for part in range(3):
                piece = parts[:, SUMS_AT + part : SUMS_AT + part + 1]
                tile = jnp.where(lane == 64 * k + 8 * part + g, piece, tile)
    return tile.astype(BF16)


def away_kernel(place_ref, gate_ref, up_ref, out_ref, sem):
    units, width = gate_ref.shape[0], out_ref.shape[1] // 8
    copies = []
    for q in range(8):
        block = pl.ds(pl.multiple_of((2 * q + 1 - place_ref[8]) * width, 128), width)
        for k, weight in enumerate((gate_ref, up_ref)):
            to = out_ref.at[pl.ds(k * units, units), pl.ds(q * width, width)]
            copies.append(pltpu.make_async_copy(weight.at[:, block], to, sem.at[q, k]))
    for copy in copies:
        copy.start()
    finish(copies)


def away_weights(place, gate_weight, up_weight):
    units, depth = gate_weight.shape
    return pl.pallas_call(
        away_kernel,
        out_shape=jax.ShapeDtypeStruct((2 * units, depth // 2), BF16),
        in_specs=[IN_SMEM, IN_HBM, IN_HBM],
        out_specs=IN_VMEM,
        scratch_shapes=[pltpu.SemaphoreType.DMA((8, 2))],
        compiler_params=pltpu.CompilerParams(vmem_limit_bytes=VMEM_LIMIT),
        cost_estimate=BRIEF,
        name="away_weights",
    )(place, gate_weight, up_weight)


def place_terms(place, grads, other_grads, gate_weight, up_weight, other_weights, groups):
    rows = grads.shape[0]
    units, depth = gate_weight.shape
    width = depth // 16
    span = rows // groups + SPARE
    return pl.pallas_call(
        terms_kernel,
        out_shape=jax.ShapeDtypeStruct((groups, 8, span, width), BF16),
        in_specs=[IN_SMEM] + [IN_HBM] * 5,
        out_specs=IN_HBM,
        scratch_shapes=[
            pltpu.VMEM((rows, 4 * GAP), BF16),
            pltpu.VMEM((4, 4 * GAP, 2 * width), BF16),
            pltpu.VMEM((4, groups, span, 2 * width), BF16),
            pltpu.SemaphoreType.DMA((2,)),
            pltpu.SemaphoreType.DMA((4, 6)),
            pltpu.SemaphoreType.DMA((4, 2)),
        ],
        compiler_params=pltpu.CompilerParams(vmem_limit_bytes=VMEM_LIMIT),
        cost_estimate=BRIEF,
        name="place_terms",
    )(place, grads, other_grads, gate_weight, up_weight, other_weights)


IN_HBM = pl.BlockSpec(memory_space=pl.ANY)
IN_VMEM = pl.BlockSpec(memory_space=pltpu.VMEM)
IN_SMEM = pl.BlockSpec(memory_space=pltpu.SMEM)


def dense(place, first, mine, other, weights, before, scale=None):
    last = scale is not None
    rows, both = mine[0].shape
    units, depth = weights[0].shape
    count = len(mine)
    shapes = [jax.ShapeDtypeStruct((rows, 2 * GAP), F32), jax.ShapeDtypeStruct((rows, units), F32)]
    kept, carried, extra = [], before, []
    if last:
        kept = [pltpu.VMEM(s.shape, F32) for s in shapes] + [pltpu.SemaphoreType.DMA((2,))]
        shapes = [jax.ShapeDtypeStruct(s.shape, BF16) for s in shapes]
        carried, extra = (*before, scale), [IN_HBM, IN_HBM, IN_VMEM]
    return pl.pallas_call(
        lambda *refs: dense_kernel(first, count, last, *refs),
        out_shape=tuple(shapes),
        in_specs=[IN_SMEM] + [IN_HBM] * (2 * count + 3) + extra,
        out_specs=[IN_VMEM] * 2,
        scratch_shapes=kept
        + [
            pltpu.VMEM((count, rows, both), BF16),
            pltpu.VMEM((count, rows, both), BF16),
            pltpu.VMEM((count, 2 * GAP, both), BF16),
            pltpu.VMEM((count, units, both), BF16),
            pltpu.SemaphoreType.DMA((count, 10)),
        ],
        compiler_params=pltpu.CompilerParams(vmem_limit_bytes=VMEM_LIMIT),
        cost_estimate=BRIEF,
        name="dense",
    )(place, *mine, *other, *weights, *carried)


def weight_kernel(place_ref, *refs):
    chunks, refs = (refs[:8], refs[8:16]), refs[16:]
    lefts, scale_ref, outs = refs[:2], refs[2], (refs[3:5], refs[5:6])
    rows_buf, both_buf, down_buf, sem, out_sem = refs[6:]
    width = chunks[0][0].shape[1] // 2
    units = outs[0][0].shape[0]
    loads, stores = [], []
    for part, out_buf in enumerate((both_buf, down_buf)):
        for j in range(8):
            load, store = [], []
            for side, block in enumerate(column_blocks(place_ref, j, width)):
                to = pl.ds(side * width, width)
                source = chunks[side][j].at[:, pl.ds(part * width, width)]
                load.append(pltpu.make_async_copy(source, rows_buf.at[part, j, :, to], sem.at[part, j, side]))
                for k, out in enumerate(outs[part]):
                    result = out_buf.at[j, pl.ds(k * GAP, units), to]
                    store.append(
                        pltpu.make_async_copy(result, out.at[:, block], out_sem.at[part, j, 2 * side + k])
                    )
            loads.append(load)
            stores.append(store)
    begin(loads, -1)
    for part, out_buf in enumerate((both_buf, down_buf)):
        step = out_buf.shape[1] // 3
        for j in range(8):
            finish(loads[8 * part + j])
            begin(loads, 8 * part + j)
            if part:
                rows_buf[1, j] = (scale_ref[...] * rows_buf[1, j].astype(F32)).astype(BF16)
            for i in range(3):
                at = pl.ds(i * step, step)
                total = jnp.dot(lefts[part][at, :], rows_buf[part, j], preferred_element_type=F32)
                out_buf[j, at, :] = total.astype(BF16)
            for copy in stores[8 * part + j]:
                copy.start()
    for group in stores:
        finish(group)


def weight_grads(place, mine, other, grads, hidden, scale):
    rows, both = mine[0].shape
    units = hidden.shape[0]
    shape = jax.ShapeDtypeStruct((units, 8 * both), BF16)
    return pl.pallas_call(
        weight_kernel,
        out_shape=(shape,) * 3,
        in_specs=[IN_SMEM] + [IN_HBM] * 16 + [IN_VMEM] * 3,
        out_specs=[IN_HBM] * 3,
        scratch_shapes=[
            pltpu.VMEM((2, 8, rows, both), BF16),
            pltpu.VMEM((8, GAP + units, both), BF16),
            pltpu.VMEM((8, units, both), BF16),
            pltpu.SemaphoreType.DMA((2, 8, 2)),
            pltpu.SemaphoreType.DMA((2, 8, 4)),
        ],
        compiler_params=pltpu.CompilerParams(vmem_limit_bytes=VMEM_LIMIT),
        cost_estimate=BRIEF,
        name="weight_grads",
    )(place, *mine, *other, grads, hidden, scale)


def shards(tokens, expert_ids, gate_values, out_grad, gate_weight, up_weight, down_weight):
    groups, lanes = lax.axis_size("expert"), lax.axis_size("etp")
    block_rows, top_count = expert_ids.shape
    own_rows, depth = tokens.shape
    width = depth // lanes
    most_rows = min(block_rows, 5 * block_rows * top_count // (4 * groups))
    capacity = groups * most_rows
    gate_weight, up_weight, down_weight = gate_weight[0], up_weight[0], down_weight[0]

    me = lax.axis_index("etp")
    x, z, core = me // 8, (me // 2) % 4, me % 2
    place = jnp.stack([(x ^ fx) * 4 + (z + sz) % 4 for fx, sz in PLACES]).astype(jnp.int32)

    chosen = expert_ids[:, :, None] == jnp.arange(groups, dtype=jnp.int32)
    routed = jnp.any(chosen, axis=1)
    share = jnp.sum(jnp.where(chosen, gate_values[:, :, None], 0.0), axis=1)
    earlier = jnp.tril(jnp.ones((block_rows, block_rows), BF16), -1)
    slot = jnp.dot(earlier, routed.astype(BF16), preferred_element_type=F32).astype(jnp.int32)
    slot = jnp.where(routed, slot, -1)
    fills = slot.T[:, None, :] == jnp.arange(most_rows, dtype=jnp.int32)[None, :, None]
    slot_weights = jnp.sum(jnp.where(fills, share.T[:, None, :], 0.0), axis=2)
    pick = fills.astype(BF16).reshape(capacity, block_rows)

    both = jnp.concatenate(
        [tokens.reshape(own_rows, lanes, width), out_grad.reshape(own_rows, lanes, width)], axis=2
    )
    columns = lax.all_to_all(both.transpose(1, 0, 2), "etp", 0, 0)
    columns = columns.reshape(block_rows, 2 * width)
    place = jnp.concatenate([place, core[None].astype(jnp.int32)])
    gate_weight, up_weight = gate_weight.T, up_weight.T
    columns, away = tie(columns, away_weights(place, gate_weight, up_weight))
    packed = jnp.dot(pick, columns, preferred_element_type=F32).astype(BF16)
    received = lax.all_to_all(packed.reshape(groups, most_rows, 2 * width), "expert", 0, 0)
    received = received.reshape(capacity, 2 * width)

    def weights_of(chunk):
        parts = jnp.pad(jnp.stack(parts_of(slot_weights), axis=1), ((0, 0), (0, 13), (0, 128 - most_rows)))
        parts, _ = tie(parts, chunk)
        parts = lax.all_to_all(parts, "expert", 0, 0)[:, :3, :most_rows].astype(F32)
        return jnp.sum(parts, axis=1).reshape(capacity, 1), move(away, CORE)

    every_weight = (gate_weight, up_weight, down_weight)
    near, near_other, onward, (weights, other_weights) = gather_near(received, weights_of)
    sums = dense(place, 0, near, near_other, every_weight, ())
    far_low, far_high, across_above, across_below = onward
    far_low, far_high, *sums = tie(far_low, far_high, *sums)
    far = jnp.concatenate([far_low, far_high], axis=0)
    across_far, far_other = move(far, ACROSS), move(far, CORE)
    across_above, across_below, far_other = tie(across_above, across_below, far_other)
    distant = [far, across_above, across_below, across_far]
    distant_other = [far_other] + [move(part, CORE) for part in distant[1:]]
    grads, hidden = dense(place, 4, distant, distant_other, every_weight, sums, weights)
    terms = place_terms(place, grads, move(grads, CORE), gate_weight, up_weight, other_weights, groups)
    gate_grad, up_grad, down_grad = weight_grads(
        place, near + distant, near_other + distant_other, grads.T, hidden.T, weights
    )

    terms = terms.reshape(groups * 8, most_rows + SPARE, width)
    peers = [[e * lanes + 2 * p + c for e in range(groups) for p in range(8)] for c in range(2)]
    back = lax.all_to_all(terms, ("expert", "etp"), 0, 0, axis_index_groups=peers)
    back = jnp.sum(back.reshape(groups, 8, most_rows + SPARE, width).astype(F32), axis=1)
    own_input = lax.dot_general(
        pick,
        back[:, :most_rows].astype(BF16).reshape(capacity, width),
        (((0,), (0,)), ((), ())),
        preferred_element_type=F32,
    ).astype(BF16)
    slot_sums = back[:, most_rows:, :128].reshape(groups, SPARE, 2, 8, 8)
    slot_sums = jnp.sum(slot_sums, axis=(2, 3))[:, :, : most_rows // SPARE]
    slot_sums = slot_sums.transpose(0, 2, 1).reshape(groups, most_rows, 1)
    token_sums = jnp.sum(jnp.where(fills, slot_sums, 0.0), axis=1)
    own_gates = jnp.sum(jnp.where(chosen, token_sums.T[:, None, :], 0.0), axis=2)
    return own_input, own_gates, gate_grad.T[None], up_grad.T[None], down_grad[None]


def solution(mesh):
    placed = (
        P(("expert", "etp"), None),
        P("expert", None),
        P("expert", None),
        P(("expert", "etp"), None),
        P("expert", None, "etp"),
        P("expert", None, "etp"),
        P("expert", "etp", None),
    )
    return jax.shard_map(
        shards,
        mesh=mesh,
        in_specs=placed,
        out_specs=(
            P("expert", "etp"),
            P("expert", None),
            P("expert", None, "etp"),
            P("expert", None, "etp"),
            P("expert", "etp", None),
        ),
        check_vma=False,
    )
```

```python
import jax
import jax.numpy as jnp
from jax import lax
from jax.experimental import pallas as pl
from jax.experimental.pallas import tpu as pltpu
from jax.sharding import PartitionSpec as P

BF16 = jnp.bfloat16
F32 = jnp.float32
VMEM_LIMIT = 56 * 1024 * 1024
GAP = 384
SPARE = 16
SUMS_AT = 80
BRIEF = pl.CostEstimate(flops=1, bytes_accessed=1, transcendentals=0)
PLACES = ((0, 0), (0, 1), (0, -1), (1, 0), (0, 2), (1, 1), (1, -1), (1, 2))


def etp_index(x, z, core):
    return x * 8 + (z % 4) * 2 + core


def etp_moves(flip_x, step_z, flip_core):
    return [
        (etp_index(x, z, c), etp_index(x ^ flip_x, z + step_z, c ^ flip_core))
        for x in range(2)
        for z in range(4)
        for c in range(2)
    ]


CORE = etp_moves(0, 0, 1)
UP = etp_moves(0, 1, 0)
DOWN = etp_moves(0, -1, 0)
ACROSS = etp_moves(1, 0, 0)


def move(value, moves):
    return lax.ppermute(value, "etp", moves)


def tie(first, *others):
    return lax.optimization_barrier((first, *others))


def gather_near(chunk, local):
    half = chunk.shape[0] // 2
    from_below, from_above, across = move(chunk, UP), move(chunk, DOWN), move(chunk, ACROSS)
    beside = move(chunk, CORE)
    from_below, from_above, across, beside, *local = tie(from_below, from_above, across, beside, *local(chunk))
    onward = (
        move(from_below[:half], UP),
        move(from_above[half:], DOWN),
        move(across, DOWN),
        move(across, UP),
    )
    mine = [chunk, from_above, from_below, across]
    return mine, [beside] + [move(part, CORE) for part in mine[1:]], onward, local


def begin(groups, now):
    for group in groups[:2] if now < 0 else groups[now + 2 : now + 3]:
        for copy in group:
            copy.start()


def finish(group):
    for copy in group:
        copy.wait()


def column_blocks(place_ref, at, width):
    core = place_ref[8]
    first = place_ref[at] * 2
    return [pl.ds(pl.multiple_of((first + side) * width, 128), width) for side in (core, 1 - core)]


def dense_kernel(first, count, last, place_ref, *refs):
    chunks, refs = (refs[:count], refs[count : 2 * count]), refs[2 * count :]
    weights, refs = refs[:3], refs[3:]
    if last:
        before, grads_ref, hidden_ref = refs[:2], refs[2], refs[3]
        both_ref, raw_ref, before_sem = refs[4:7]
        refs = refs[7:]
    else:
        both_ref, raw_ref = refs[:2]
        refs = refs[2:]
    rows_buf, out_buf, both_buf, down_buf, sem = refs
    width = chunks[0][0].shape[1] // 2
    units = weights[0].shape[0]
    loads = []
    for j in range(count):
        pairs = []
        for side, block in enumerate(column_blocks(place_ref, first + j, width)):
            to = pl.ds(side * width, width)
            pairs.append((weights[0].at[:, block], both_buf.at[j, pl.ds(0, units), to]))
            pairs.append((weights[1].at[:, block], both_buf.at[j, pl.ds(GAP, units), to]))
            pairs.append((weights[2].at[:, block], down_buf.at[j, :, to]))
            pairs.append((chunks[side][j].at[:, pl.ds(0, width)], rows_buf.at[j, :, to]))
            pairs.append((chunks[side][j].at[:, pl.ds(width, width)], out_buf.at[j, :, to]))
        loads.append([pltpu.make_async_copy(s, d, sem.at[j, k]) for k, (s, d) in enumerate(pairs)])
    begin(loads, -1)
    if last:
        carried = [
            pltpu.make_async_copy(source, to, before_sem.at[k])
            for k, (source, to) in enumerate(zip(before, (both_ref, raw_ref)))
        ]
        for copy in carried:
            copy.start()
    blank = jnp.zeros((both_buf.shape[0], GAP - units, 2 * width), BF16)
    both_buf[:, units:GAP, :] = blank
    both_buf[:, GAP + units :, :] = blank
    across = (((1,), (1,)), ((), ()))
    for j in range(count):
        finish(loads[j])
        begin(loads, j)
        both_part = lax.dot_general(rows_buf[j], both_buf[j], across, preferred_element_type=F32)
        raw_part = lax.dot_general(out_buf[j], down_buf[j], across, preferred_element_type=F32)
        if last and j == 0:
            finish(carried)
        if last or j:
            both_ref[...] += both_part
            raw_ref[...] += raw_part
        else:
            both_ref[...] = both_part
            raw_ref[...] = raw_part

    if last:
        step = 80

        @pl.loop(0, raw_ref.shape[0] // step)
        def _(i):
            rows = pl.ds(pl.multiple_of(i * step, step), step)
            gate, up, raw = both_ref[rows, :units], both_ref[rows, GAP : GAP + units], raw_ref[rows, :]
            sigmoid = jax.nn.sigmoid(gate)
            active = gate * sigmoid
            hidden = (active * up).astype(BF16)
            hidden_ref[rows, :] = hidden
            rest = jnp.sum(hidden.astype(F32) * raw, axis=1, keepdims=True)
            lane = lax.broadcasted_iota(jnp.int32, (step, GAP - units), 1)
            sums = jnp.zeros((step, GAP - units), F32)
            for part in range(3):
                piece = rest.astype(BF16).astype(F32)
                sums = jnp.where(lane == part, piece, sums)
                rest = rest - piece
            grad_gate = raw * up * sigmoid * (1.0 + gate * (1.0 - sigmoid))
            grads_ref[rows, units:GAP] = jnp.zeros((step, GAP - units), BF16)
            grads_ref[rows, GAP + units :] = sums.astype(BF16)
            grads_ref[rows, :units] = grad_gate.astype(BF16)
            grads_ref[rows, GAP : GAP + units] = (raw * active).astype(BF16)


def terms_kernel(place_ref, grads_ref, other_grads_ref, gate_ref, up_ref, other_ref, out_ref, *scratch):
    grads_buf, weight_buf, terms_buf, grads_sem, sem, terms_sem = scratch
    width = out_ref.shape[3]
    units = gate_ref.shape[0]
    span = 2 * GAP
    core = place_ref[8]
    step = out_ref.shape[2] - SPARE
    both = [
        pltpu.make_async_copy(source, grads_buf.at[:, pl.ds(k * span, span)], grads_sem.at[k])
        for k, source in enumerate((grads_ref, other_grads_ref))
    ]
    for copy in both:
        copy.start()
    loads = []
    for j in range(4):
        pairs = []
        for side in range(2):
            block = pl.ds(pl.multiple_of((2 * (2 * j + side) + core) * width, 128), width)
            to = pl.ds(side * width, width)
            pairs.append((gate_ref.at[:, block], weight_buf.at[j, pl.ds(0, units), to]))
            pairs.append((up_ref.at[:, block], weight_buf.at[j, pl.ds(GAP, units), to]))
        block = pl.ds(2 * j * width, 2 * width)
        for k in range(2):
            rows = pl.ds(span + k * GAP, units)
            pairs.append((other_ref.at[pl.ds(k * units, units), block], weight_buf.at[j, rows, :]))
        loads.append([pltpu.make_async_copy(s, d, sem.at[j, k]) for k, (s, d) in enumerate(pairs)])
    begin(loads, -1)
    for k in range(4):
        weight_buf[:, k * GAP + units : (k + 1) * GAP, :] = jnp.zeros((4, GAP - units, 2 * width), BF16)
    finish(both)
    stores = []
    for j in range(4):
        finish(loads[j])
        begin(loads, j)
        for i in range(terms_buf.shape[1] // 2):
            rows = pl.ds(2 * i * step, 2 * step)
            total = jnp.dot(grads_buf[rows, :], weight_buf[j], preferred_element_type=F32).astype(BF16)
            terms_buf[j, 2 * i, :step, :] = total[:step]
            terms_buf[j, 2 * i + 1, :step, :] = total[step:]
        for i in range(terms_buf.shape[1]):
            terms_buf[j, i, step:, :] = jnp.zeros((SPARE, 2 * width), BF16)
            tile = spare_rows(grads_buf, i * step, step) if j == 0 else terms_buf[0, i, step:, :128]
            terms_buf[j, i, step:, :128] = tile
            terms_buf[j, i, step:, width : width + 128] = tile
        group = [
            pltpu.make_async_copy(
                terms_buf.at[j, :, :, pl.ds(side * width, width)], out_ref.at[:, 2 * j + side], terms_sem.at[j, side]
            )
            for side in range(2)
        ]
        for copy in group:
            copy.start()
        stores.append(group)
    for group in stores:
        finish(group)


def spare_rows(grads_buf, start, count):
    lane = lax.broadcasted_iota(jnp.int32, (SPARE, 128), 1)
    tile = jnp.zeros((SPARE, 128), F32)
    for k in range(2):
        end = 2 * GAP * (k + 1)
        for g in range(count // SPARE):
            parts = grads_buf[pl.ds(start + g * SPARE, SPARE), end - 128 : end].astype(F32)
            for part in range(3):
                piece = parts[:, SUMS_AT + part : SUMS_AT + part + 1]
                tile = jnp.where(lane == 64 * k + 8 * part + g, piece, tile)
    return tile.astype(BF16)


def away_kernel(place_ref, gate_ref, up_ref, out_ref, sem):
    units, width = gate_ref.shape[0], out_ref.shape[1] // 8
    copies = []
    for q in range(8):
        block = pl.ds(pl.multiple_of((2 * q + 1 - place_ref[8]) * width, 128), width)
        for k, weight in enumerate((gate_ref, up_ref)):
            to = out_ref.at[pl.ds(k * units, units), pl.ds(q * width, width)]
            copies.append(pltpu.make_async_copy(weight.at[:, block], to, sem.at[q, k]))
    for copy in copies:
        copy.start()
    finish(copies)


def away_weights(place, gate_weight, up_weight):
    units, depth = gate_weight.shape
    return pl.pallas_call(
        away_kernel,
        out_shape=jax.ShapeDtypeStruct((2 * units, depth // 2), BF16),
        in_specs=[IN_SMEM, IN_HBM, IN_HBM],
        out_specs=IN_VMEM,
        scratch_shapes=[pltpu.SemaphoreType.DMA((8, 2))],
        compiler_params=pltpu.CompilerParams(vmem_limit_bytes=VMEM_LIMIT),
        cost_estimate=BRIEF,
        name="away_weights",
    )(place, gate_weight, up_weight)


def place_terms(place, grads, other_grads, gate_weight, up_weight, other_weights, groups):
    rows = grads.shape[0]
    units, depth = gate_weight.shape
    width = depth // 16
    span = rows // groups + SPARE
    return pl.pallas_call(
        terms_kernel,
        out_shape=jax.ShapeDtypeStruct((groups, 8, span, width), BF16),
        in_specs=[IN_SMEM] + [IN_HBM] * 5,
        out_specs=IN_HBM,
        scratch_shapes=[
            pltpu.VMEM((rows, 4 * GAP), BF16),
            pltpu.VMEM((4, 4 * GAP, 2 * width), BF16),
            pltpu.VMEM((4, groups, span, 2 * width), BF16),
            pltpu.SemaphoreType.DMA((2,)),
            pltpu.SemaphoreType.DMA((4, 6)),
            pltpu.SemaphoreType.DMA((4, 2)),
        ],
        compiler_params=pltpu.CompilerParams(vmem_limit_bytes=VMEM_LIMIT),
        cost_estimate=BRIEF,
        name="place_terms",
    )(place, grads, other_grads, gate_weight, up_weight, other_weights)


IN_HBM = pl.BlockSpec(memory_space=pl.ANY)
IN_VMEM = pl.BlockSpec(memory_space=pltpu.VMEM)
IN_SMEM = pl.BlockSpec(memory_space=pltpu.SMEM)


def dense(place, first, mine, other, weights, before):
    last = len(before) > 0
    rows, both = mine[0].shape
    units, depth = weights[0].shape
    count = len(mine)
    shapes = [jax.ShapeDtypeStruct((rows, 2 * GAP), F32), jax.ShapeDtypeStruct((rows, units), F32)]
    kept, carried, extra = [], before, []
    if last:
        kept = [pltpu.VMEM(s.shape, F32) for s in shapes] + [pltpu.SemaphoreType.DMA((2,))]
        shapes = [jax.ShapeDtypeStruct(s.shape, BF16) for s in shapes]
        extra = [IN_HBM, IN_HBM]
    return pl.pallas_call(
        lambda *refs: dense_kernel(first, count, last, *refs),
        out_shape=tuple(shapes),
        in_specs=[IN_SMEM] + [IN_HBM] * (2 * count + 3) + extra,
        out_specs=[IN_VMEM] * 2,
        scratch_shapes=kept
        + [
            pltpu.VMEM((count, rows, both), BF16),
            pltpu.VMEM((count, rows, both), BF16),
            pltpu.VMEM((count, 2 * GAP, both), BF16),
            pltpu.VMEM((count, units, both), BF16),
            pltpu.SemaphoreType.DMA((count, 10)),
        ],
        compiler_params=pltpu.CompilerParams(vmem_limit_bytes=VMEM_LIMIT),
        cost_estimate=BRIEF,
        name="dense",
    )(place, *mine, *other, *weights, *carried)


def weight_kernel(place_ref, *refs):
    chunks, refs = (refs[:8], refs[8:16]), refs[16:]
    lefts, outs = refs[:2], (refs[2:4], refs[4:5])
    rows_buf, both_buf, down_buf, sem, out_sem = refs[5:]
    width = chunks[0][0].shape[1] // 2
    units = outs[0][0].shape[0]
    loads, stores = [], []
    for part, out_buf in enumerate((both_buf, down_buf)):
        for j in range(8):
            load, store = [], []
            for side, block in enumerate(column_blocks(place_ref, j, width)):
                to = pl.ds(side * width, width)
                source = chunks[side][j].at[:, pl.ds(part * width, width)]
                load.append(pltpu.make_async_copy(source, rows_buf.at[part, j, :, to], sem.at[part, j, side]))
                for k, out in enumerate(outs[part]):
                    result = out_buf.at[j, pl.ds(k * GAP, units), to]
                    store.append(
                        pltpu.make_async_copy(result, out.at[:, block], out_sem.at[part, j, 2 * side + k])
                    )
            loads.append(load)
            stores.append(store)
    begin(loads, -1)
    for part, out_buf in enumerate((both_buf, down_buf)):
        step = out_buf.shape[1] // 3
        for j in range(8):
            finish(loads[8 * part + j])
            begin(loads, 8 * part + j)
            for i in range(3):
                at = pl.ds(i * step, step)
                total = jnp.dot(lefts[part][at, :], rows_buf[part, j], preferred_element_type=F32)
                out_buf[j, at, :] = total.astype(BF16)
            for copy in stores[8 * part + j]:
                copy.start()
    for group in stores:
        finish(group)


def weight_grads(place, mine, other, grads, hidden):
    rows, both = mine[0].shape
    units = hidden.shape[0]
    shape = jax.ShapeDtypeStruct((units, 8 * both), BF16)
    return pl.pallas_call(
        weight_kernel,
        out_shape=(shape,) * 3,
        in_specs=[IN_SMEM] + [IN_HBM] * 16 + [IN_VMEM] * 2,
        out_specs=[IN_HBM] * 3,
        scratch_shapes=[
            pltpu.VMEM((2, 8, rows, both), BF16),
            pltpu.VMEM((8, GAP + units, both), BF16),
            pltpu.VMEM((8, units, both), BF16),
            pltpu.SemaphoreType.DMA((2, 8, 2)),
            pltpu.SemaphoreType.DMA((2, 8, 4)),
        ],
        compiler_params=pltpu.CompilerParams(vmem_limit_bytes=VMEM_LIMIT),
        cost_estimate=BRIEF,
        name="weight_grads",
    )(place, *mine, *other, grads, hidden)


def shards(tokens, expert_ids, gate_values, out_grad, gate_weight, up_weight, down_weight):
    groups, lanes = lax.axis_size("expert"), lax.axis_size("etp")
    block_rows, top_count = expert_ids.shape
    own_rows, depth = tokens.shape
    width = depth // lanes
    most_rows = min(block_rows, 5 * block_rows * top_count // (4 * groups))
    capacity = groups * most_rows
    gate_weight, up_weight, down_weight = gate_weight[0], up_weight[0], down_weight[0]

    me = lax.axis_index("etp")
    x, z, core = me // 8, (me // 2) % 4, me % 2
    place = jnp.stack([(x ^ fx) * 4 + (z + sz) % 4 for fx, sz in PLACES]).astype(jnp.int32)

    chosen = expert_ids[:, :, None] == jnp.arange(groups, dtype=jnp.int32)
    routed = jnp.any(chosen, axis=1)
    share = jnp.sum(jnp.where(chosen, gate_values[:, :, None], 0.0), axis=1)
    earlier = jnp.tril(jnp.ones((block_rows, block_rows), BF16), -1)
    slot = jnp.dot(earlier, routed.astype(BF16), preferred_element_type=F32).astype(jnp.int32)
    slot = jnp.where(routed, slot, -1)
    fills = slot.T[:, None, :] == jnp.arange(most_rows, dtype=jnp.int32)[None, :, None]
    slot_weights = jnp.sum(jnp.where(fills, share.T[:, None, :], 0.0), axis=2)
    pick = fills.astype(BF16).reshape(capacity, block_rows)

    both = jnp.concatenate(
        [tokens.reshape(own_rows, lanes, width), out_grad.reshape(own_rows, lanes, width)], axis=2
    )
    columns = lax.all_to_all(both.transpose(1, 0, 2), "etp", 0, 0)
    columns = columns.reshape(block_rows, 2 * width)
    place = jnp.concatenate([place, core[None].astype(jnp.int32)])
    gate_weight, up_weight = gate_weight.T, up_weight.T
    columns, away = tie(columns, away_weights(place, gate_weight, up_weight))
    packed = jnp.dot(pick, columns, preferred_element_type=F32)
    in_grads = jnp.arange(2 * width) >= width
    packed = (packed * jnp.where(in_grads, slot_weights.reshape(capacity, 1), 1.0)).astype(BF16)
    received = lax.all_to_all(packed.reshape(groups, most_rows, 2 * width), "expert", 0, 0)
    received = received.reshape(capacity, 2 * width)

    every_weight = (gate_weight, up_weight, down_weight)
    near, near_other, onward, (other_weights,) = gather_near(received, lambda _: [move(away, CORE)])
    sums = dense(place, 0, near, near_other, every_weight, ())
    far_low, far_high, across_above, across_below = onward
    far = jnp.concatenate([far_low, far_high], axis=0)
    across_far, far_other = move(far, ACROSS), move(far, CORE)
    across_above, across_below, far_other, *sums = tie(across_above, across_below, far_other, *sums)
    distant = [far, across_above, across_below, across_far]
    distant_other = [far_other] + [move(part, CORE) for part in distant[1:]]
    grads, hidden = dense(place, 4, distant, distant_other, every_weight, sums)
    terms = place_terms(place, grads, move(grads, CORE), gate_weight, up_weight, other_weights, groups)
    gate_grad, up_grad, down_grad = weight_grads(
        place, near + distant, near_other + distant_other, grads.T, hidden.T
    )

    terms = terms.reshape(groups * 8, most_rows + SPARE, width)
    peers = [[e * lanes + 2 * p + c for e in range(groups) for p in range(8)] for c in range(2)]
    back = lax.all_to_all(terms, ("expert", "etp"), 0, 0, axis_index_groups=peers)
    back = jnp.sum(back.reshape(groups, 8, most_rows + SPARE, width).astype(F32), axis=1)
    own_input = lax.dot_general(
        pick,
        back[:, :most_rows].astype(BF16).reshape(capacity, width),
        (((0,), (0,)), ((), ())),
        preferred_element_type=F32,
    ).astype(BF16)
    slot_sums = back[:, most_rows:, :128].reshape(groups, SPARE, 2, 8, 8)
    slot_sums = jnp.sum(slot_sums, axis=(2, 3))[:, :, : most_rows // SPARE]
    slot_sums = slot_sums.transpose(0, 2, 1).reshape(groups, most_rows, 1)
    token_sums = jnp.sum(jnp.where(fills, slot_sums, 0.0), axis=1)
    own_gates = jnp.sum(jnp.where(chosen, token_sums.T[:, None, :], 0.0), axis=2) / gate_values
    return own_input, own_gates, gate_grad.T[None], up_grad.T[None], down_grad[None]


def solution(mesh):
    placed = (
        P(("expert", "etp"), None),
        P("expert", None),
        P("expert", None),
        P(("expert", "etp"), None),
        P("expert", None, "etp"),
        P("expert", None, "etp"),
        P("expert", "etp", None),
    )
    return jax.shard_map(
        shards,
        mesh=mesh,
        in_specs=placed,
        out_specs=(
            P("expert", "etp"),
            P("expert", None),
            P("expert", None, "etp"),
            P("expert", None, "etp"),
            P("expert", "etp", None),
        ),
        check_vma=False,
    )
```
